128 devices in a mesh: rep: 8 (over x, z_lo), blk: 16 (over y, z_hi, core).
Axes of the slice: x: 4, y: 4, z: 4 (z_hi: 2, z_lo: 2; z = z_hi * 2 + z_lo), core: 2. Of those that a mesh axis runs over, the one named last changes fastest.
Arguments:
- acts: bfloat16 [4096, 8192], P('rep', 'blk'), may hold values from -6 to 6
- out_grads: bfloat16 [4096, 1024], P('rep'), may hold values from -0.119628906 to 0.119628906
- codes: bfloat16 [8192, 8192], P('blk'), may hold values from -127 to 127, as said below
- scales: float32 [64, 64], P('blk')
- old_factor: float32 [8192, 8192], P('rep', 'blk'), may hold values from -0.12 to 0.12
- due: int32 [64, 64], P('rep', 'blk'), may hold values 0 or 1
Outputs:
- precond: bfloat16 [8192, 1024], P('blk')
- new_factor: float32 [8192, 8192], P('rep', 'blk')
The draws below stay inside these ranges and needn't reach their ends.
Inputs may be any that keep to these rules, and one draw needn't show every extreme that they name: codes are whole numbers, and codes and scales are symmetric matrices.
All inputs are finite; a program needn't handle non-finite values. No bound on the sum of `due` on one device may be relied on, other than what follows from the above.
Results may differ from the reference program's by a relative error of at most 0.012.
Values may be sent and summed in bfloat16 or wider, within the bound.
A program may use at most 192 MiB of HBM per device.

```python
import jax
import jax.numpy as jnp

D = 8192
QB = 128
BAND = 1024
TOKENS = 4096


def symmetric(matrix):
    rows = lax_rows(matrix.shape[0])
    return jnp.where(rows <= rows.T, matrix, matrix.T)


def lax_rows(count):
    return jnp.arange(count, dtype=jnp.int32)[:, None] + jnp.zeros((1, count), jnp.int32)


def draw_codes(key, part):
    key = jax.random.fold_in(key, 11)
    raw = jax.random.randint(key, (D, D), -127, 128)
    return symmetric(raw).astype(jnp.bfloat16)


def draw_scales(key, part):
    key = jax.random.fold_in(key, 23)
    count = D // QB
    lower, upper = (5e-05, 0.0005)
    spread = jax.random.uniform(key, (count, count), jnp.float32, jnp.log(lower), jnp.log(upper))
    return jnp.exp(symmetric(spread))


def place_ends(result, key, low, high):
    place = [jax.random.randint(jax.random.fold_in(key, axis), (), 0, length) for axis, length in enumerate(result.shape)]
    widest = result.shape.index(max(result.shape))
    next_to = place[:widest] + [(place[widest] + 1) % result.shape[widest]] + place[widest + 1:]
    return result.at[tuple(place)].set(low).at[tuple(next_to)].set(high)


def block_levels(own_key, extent, shards, low, largest):
    loudness, own = 1.0, jax.random.fold_in(own_key, 6)
    for position, parts in shards:
        heights = jnp.exp(jax.random.uniform(jax.random.fold_in(own, position), (parts,), jnp.float32, low / len(shards), largest / len(shards)))
        loudness = loudness * jnp.repeat(heights, extent[position] // parts).reshape([-1 if axis == position else 1 for axis in range(len(extent))])
    return loudness


def normal_values(stream_key, extent, width, limit, pieces=(), kind=jnp.bfloat16):
    values = width * jax.random.normal(stream_key, extent, jnp.float32)
    if pieces:
        values = values * block_levels(stream_key, extent, pieces, -0.22, 0.18)
    return jnp.clip(values, -limit, limit).astype(kind)


def setup_inputs(seed: int = 0) -> dict:
    seeds = jax.random.split(jax.random.key(seed), 7)
    return {
        "acts": normal_values(seeds[0], (TOKENS, D), 1.0, 6.0, ((0, 8), (1, 16))),
        "out_grads": normal_values(seeds[1], (TOKENS, BAND), 0.02, 0.119628906, ((0, 8),)),
        "codes": draw_codes(jax.random.fold_in(seeds[6], 71), 0),
        "scales": draw_scales(jax.random.fold_in(seeds[6], 71), 0),
        "old_factor": normal_values(seeds[4], (D, D), 0.02, 0.12, ((0, 8), (1, 16)), jnp.float32),
        "due": place_ends((jax.random.randint(seeds[5], (D // QB, D // QB), 0, 2) < 1).astype(jnp.int32), jax.random.fold_in(seeds[5], 1), 0, 1),
    }


def reference(acts, out_grads, codes, scales, old_factor, due):
    partial_value = jnp.dot(acts.T, out_grads, preferred_element_type=jnp.float32)
    grad = partial_value.astype(jnp.bfloat16)
    stats = jnp.dot(acts.T, acts, preferred_element_type=jnp.float32) / TOKENS
    mask_full = jnp.repeat(jnp.repeat(due, QB, axis=0), QB, axis=1)
    blend = 0.5 * old_factor + 0.5 * stats
    new_factor = jnp.where(mask_full == 1, blend, old_factor)
    scale_full = jnp.repeat(jnp.repeat(scales, QB, axis=0), QB, axis=1)
    inverse = (codes.astype(jnp.float32) * scale_full).astype(jnp.bfloat16)
    precond = jnp.dot(inverse, grad, preferred_element_type=jnp.float32).astype(jnp.bfloat16)
    return precond, new_factor
```

```python
import functools

import jax
import jax.numpy as jnp
from jax import lax
from jax.experimental import pallas as pl
from jax.experimental.pallas import tpu as pltpu
from jax.sharding import PartitionSpec as P

MESH = pl.DeviceIdType.MESH
F32, BF16 = jnp.float32, jnp.bfloat16


def tdot(left, right):
    return lax.dot_general(
        left, right, (((0,), (0,)), ((), ())), preferred_element_type=F32
    )


def kernel(
    acts, out_grads, codes, scales, old_factor, due, precond, new_factor,
    cols, rows, spread, band, partial, parts, grad, inverse, factor, stats, piece,
    send, recv, local,
):
    r, b = lax.axis_index("rep"), lax.axis_index("blk")
    x, zl = r // 2, r % 2
    y, zh, k = b // 4, (b // 2) % 2, b % 2
    z = 2 * zh + zl
    turned = 2 * zl + zh

    def device(x, y, z, k):
        return (2 * (x % 4) + z % 2, 4 * (y % 4) + 2 * (z // 2) + k)

    def along_x(step, flip=0):
        return device(x + step, y, 2 * zh + (1 - zl if flip else zl), k)

    def along_y(step):
        return device(x, y + step, z, k)

    zl_mate = along_x(0, 1)
    zh_mate = device(x, y, 2 * (1 - zh) + zl, k)
    sibling = device(x, y, z, 1 - k)

    count = [0, 0]
    started = []

    def put(src, dst, target, start=True):
        i = count[0]
        count[0] += 1
        copy = pltpu.make_async_remote_copy(
            src_ref=src, dst_ref=dst, send_sem=send.at[i], recv_sem=recv.at[i],
            device_id=target, device_id_type=MESH,
        )
        copy.start()
        started.append(copy)
        return copy

    def bring(src, dst):
        i = count[1]
        count[1] += 1
        copy = pltpu.make_async_copy(src, dst, local.at[i])
        copy.start()
        return copy

    get_acts = bring(acts, cols.at[x, zl])
    get_band = bring(out_grads, band)
    get_codes = [bring(codes.at[:, pl.ds(512 * i, 512)], inverse.at[i]) for i in range(16)]
    get_old = bring(old_factor, factor)

    barrier = pltpu.get_barrier_semaphore()
    partners = [along_x(step, flip) for flip in (0, 1) for step in range(4) if step or flip]
    partners += [along_y(step) for step in (1, 2, 3)] + [zh_mate, sibling]
    for partner in partners:
        pl.semaphore_signal(barrier, inc=1, device_id=partner, device_id_type=MESH)
    mixed = zl != zh

    @pl.when(mixed)
    def _():
        for step in range(4):
            pl.semaphore_signal(
                barrier, inc=1, device_id=device(x + step, y, turned, k), device_id_type=MESH
            )

    get_acts.wait()
    get_band.wait()
    mine = cols[x, zl].reshape(512, 512)
    for i in range(4):
        part = tdot(mine, band[:, 256 * i : 256 * i + 256]).astype(BF16)
        partial[2 * i] = part[:, :128]
        partial[2 * i + 1] = part[:, 128:]

    pl.semaphore_wait(barrier, len(partners) + 4 * (zl + zh - 2 * zl * zh))

    scatter = []
    for step, flip in ((1, 0), (3, 0), (0, 1), (1, 1), (3, 1), (2, 0), (2, 1)):
        to = 2 * ((x + step) % 4) + (1 - zl if flip else zl)
        scatter.append(put(partial.at[to], parts.at[r], along_x(step, flip)))

    spread_sends = [
        put(cols.at[x, zl, (y + step) % 4], spread.at[y], along_y(step)) for step in (1, 3, 2)
    ]
    own_quarter = bring(cols.at[x, zl, y], spread.at[y])
    cols_zl = put(cols.at[x, zl], cols.at[x, zl], zl_mate)

    stats[...] = jnp.zeros_like(stats)

    def dequantize(i):
        for u in range(4):
            for v in range(4):
                at = (i, pl.ds(128 * u, 128), pl.ds(128 * v, 128))
                inverse[at] = (inverse[at].astype(F32) * scales[u, 4 * i + v]).astype(BF16)

    def dequantize_some(first, last):
        for i in range(first, last):
            get_codes[i].wait()
        lax.fori_loop(first, last, lambda i, c: (dequantize(i), c)[1], 0)

    dequantize_some(0, 8)

    own_quarter.wait()
    for copy in spread_sends:
        copy.wait_recv()
    turns = []
    for step in (1, 3, 2):
        to = (x + step) % 4
        turns.append(put(spread.at[to], rows.at[k, x, zl, y], device(to, y, turned, k)))
    i0 = count[0]
    count[0] += 1
    stay = pltpu.make_async_copy(spread.at[x], rows.at[k, x, zl, y], recv.at[i0])
    go = pltpu.make_async_remote_copy(
        src_ref=spread.at[x], dst_ref=rows.at[k, x, zl, y], send_sem=send.at[i0],
        recv_sem=recv.at[i0], device_id=device(x, y, turned, k), device_id_type=MESH,
    )

    @pl.when(mixed)
    def _():
        go.start()

    @pl.when(jnp.logical_not(mixed))
    def _():
        stay.start()

    dequantize_some(8, 16)

    for copy in scatter:
        copy.wait_recv()
    total = partial[r].astype(F32)
    for step, flip in ((1, 0), (3, 0), (0, 1), (1, 1), (3, 1), (2, 0), (2, 1)):
        frm = 2 * ((x + step) % 4) + (1 - zl if flip else zl)
        total = total + parts[frm].astype(F32)
    grad[y, zh, k] = total.astype(BF16)
    own = grad.at[y, zh, k]
    other = grad.at[y, 1 - zh, k]
    grad_zh = put(own, own, zh_mate)
    grad_own = {step: put(own, own, along_y(step)) for step in (1, 3, 2)}

    def half(ref, h):
        return ref.at[pl.ds(2 * h, 2)]

    def both_ways(ref, plus, minus):
        sends = {}
        for h in (0, 1):
            part = half(ref, h)
            sends[1, h] = put(part, part, plus)
            sends[3, h] = put(part, part, minus)
        return sends

    cols_own = both_ways(cols.at[x, zl], along_x(1), along_x(3))

    for copy in turns:
        copy.wait_recv()
    stay.wait()

    def group(zl_of, q, h=None):
        if h is None:
            return rows.at[k, :, zl_of, q]
        return rows.at[k, pl.ds(2 * h, 2), zl_of, q]

    rows_zh = [put(group(zh, y, h), group(zh, y, h), zh_mate) for h in (0, 1)]

    def along_both(zl_of):
        sends = {}
        for h in (0, 1):
            part = group(zl_of, y, h)
            sends[1, h] = put(part, part, along_y(1))
            sends[3, h] = put(part, part, along_y(3))
        return sends

    rows_a = along_both(zh)
    share = [put(group(zh, y), group(zh, y), sibling)]

    grad_zh.wait_recv()
    grad_other = {step: put(other, other, along_y(step)) for step in (1, 3, 2)}
    pair = grad.at[y, :, k]
    grad_share = [put(pair, pair, sibling)]

    cols_zl.wait_recv()
    cols_other = both_ways(cols.at[x, 1 - zl], along_x(1), along_x(3))

    for copy in rows_zh:
        copy.wait_recv()
    rows_b = along_both(1 - zh)
    share.append(put(group(1 - zh, y), group(1 - zh, y), sibling))

    for step in (1, 3, 2):
        grad_own[step].wait_recv()
        grad_other[step].wait_recv()
        pair = grad.at[(y - step + 4) % 4, :, k]
        grad_share.append(put(pair, pair, sibling))

    def forward_rows(sends, zl_of):
        sends[1, 0].wait_recv()
        low = group(zl_of, (y + 3) % 4, 0)
        forth = put(low, low, along_y(1))
        sends[3, 1].wait_recv()
        high = group(zl_of, (y + 1) % 4, 1)
        back = put(high, high, along_y(3))
        return forth, back

    def forward_cols(sends, zl_of):
        sends[1, 0].wait_recv()
        low = half(cols.at[(x + 3) % 4, zl_of], 0)
        forth = put(low, low, along_x(1))
        sends[3, 1].wait_recv()
        high = half(cols.at[(x + 1) % 4, zl_of], 1)
        back = put(high, high, along_x(3))
        return forth, back

    far_cols_own = forward_cols(cols_own, zl)
    far_rows_a = forward_rows(rows_a, zh)

    result = jnp.zeros((512, 128), F32)
    for copy in grad_share:
        copy.wait_recv()

    def add(i, total):
        return total + jnp.dot(
            inverse[i], grad[i // 4, (i // 2) % 2, i % 2], preferred_element_type=F32
        )

    piece[...] = lax.fori_loop(0, 16, add, result).astype(BF16)

    def slot(of):
        return precond.at[:, pl.ds(pl.multiple_of(128 * of, 128), 128)]

    keep = bring(piece, slot(r))
    out_zl = put(piece, slot(r), zl_mate)
    out_own = [put(piece, slot(r), along_x(step)) for step in (1, 3, 2)]

    def share_rows(zl_of, q):
        share.append(put(group(zl_of, q), group(zl_of, q), sibling))

    def sides(sends, zl_of):
        sends[1, 1].wait_recv()
        share_rows(zl_of, (y + 3) % 4)
        sends[3, 0].wait_recv()
        share_rows(zl_of, (y + 1) % 4)

    sides(rows_a, zh)
    far_cols_other = forward_cols(cols_other, 1 - zl)
    far_rows_b = forward_rows(rows_b, 1 - zh)

    out_zl.wait_recv()
    mate = 2 * x + 1 - zl
    out_other = [put(slot(mate), slot(mate), along_x(step)) for step in (1, 3, 2)]

    for copy in far_rows_a:
        copy.wait_recv()
    share_rows(zh, (y + 2) % 4)
    sides(rows_b, 1 - zh)
    for copy in far_rows_b:
        copy.wait_recv()
    share_rows(1 - zh, (y + 2) % 4)

    for sends, far in ((cols_own, far_cols_own), (cols_other, far_cols_other)):
        sends[1, 1].wait_recv()
        sends[3, 0].wait_recv()
        for copy in far:
            copy.wait_recv()
    for copy in share:
        copy.wait_recv()

    def accumulate(i, c):
        kk, zz, q = i // 8, (i // 4) % 2, i % 4
        stats[kk] += tdot(
            rows[kk, :, zz, q].reshape(512, 512), cols[:, zz, q].reshape(512, 512)
        )
        return c

    lax.fori_loop(0, 16, accumulate, 0)

    get_old.wait()
    for i in range(8):
        for j in range(4):
            at = (pl.ds(128 * i, 128), pl.ds(128 * j, 128))
            old = factor[at]
            new = stats[i // 4, pl.ds(128 * (i % 4), 128), pl.ds(128 * j, 128)]
            blend = 0.5 * old + 0.5 * (new / 4096)
            factor[at] = jnp.where(due[i, j] == 1, blend, old)
    leave = bring(factor, new_factor)

    for copy in out_own + out_other:
        copy.wait_recv()
    for copy in started:
        copy.wait_send()

    @pl.when(mixed)
    def _():
        go.wait_send()

    keep.wait()
    leave.wait()


def local(acts, out_grads, codes, scales, old_factor, due):
    anywhere = pl.BlockSpec(memory_space=pl.ANY)
    scalar = pl.BlockSpec(memory_space=pltpu.SMEM)
    return pl.pallas_call(
        kernel,
        out_shape=(
            jax.ShapeDtypeStruct((512, 1024), BF16),
            jax.ShapeDtypeStruct((1024, 512), F32),
        ),
        in_specs=[anywhere, anywhere, anywhere, scalar, anywhere, scalar],
        out_specs=(anywhere, anywhere),
        scratch_shapes=[
            pltpu.VMEM((4, 2, 4, 128, 512), BF16),
            pltpu.VMEM((2, 4, 2, 4, 128, 512), BF16),
            pltpu.VMEM((4, 128, 512), BF16),
            pltpu.VMEM((512, 1024), BF16),
            pltpu.VMEM((8, 512, 128), BF16),
            pltpu.VMEM((8, 512, 128), BF16),
            pltpu.VMEM((4, 2, 2, 512, 128), BF16),
            pltpu.VMEM((16, 512, 512), BF16),
            pltpu.VMEM((1024, 512), F32),
            pltpu.VMEM((2, 512, 512), F32),
            pltpu.VMEM((512, 128), BF16),
            pltpu.SemaphoreType.DMA((80,)),
            pltpu.SemaphoreType.DMA((80,)),
            pltpu.SemaphoreType.DMA((24,)),
        ],
        compiler_params=pltpu.CompilerParams(
            collective_id=0, has_side_effects=True, vmem_limit_bytes=56 * 2**20
        ),
    )(acts.reshape(4, 128, 512), out_grads, codes, scales, old_factor, due)


def solution(mesh):
    return jax.shard_map(
        local,
        mesh=mesh,
        in_specs=(
            P("rep", "blk"),
            P("rep", None),
            P("blk", None),
            P("blk", None),
            P("rep", "blk"),
            P("rep", "blk"),
        ),
        out_specs=(P("blk", None), P("rep", "blk")),
        check_vma=False,
    )
```

```python
import jax
import jax.numpy as jnp
from jax import lax
from jax.experimental import pallas as pl
from jax.experimental.pallas import tpu as pltpu
from jax.sharding import PartitionSpec as P

MESH = pl.DeviceIdType.MESH
F32, BF16 = jnp.float32, jnp.bfloat16


def tdot(left, right):
    return lax.dot_general(
        left, right, (((0,), (0,)), ((), ())), preferred_element_type=F32
    )


def kernel(
    acts, out_grads, codes, scales, old_factor, due, precond, new_factor,
    cols, rows, spread, band, partial, parts, grad, inverse, factor, stats, piece,
    send, recv, local,
):
    r, b = lax.axis_index("rep"), lax.axis_index("blk")
    x, zl = r // 2, r % 2
    y, zh, k = b // 4, (b // 2) % 2, b % 2
    z = 2 * zh + zl
    turned = 2 * zl + zh
    mixed = zl != zh

    def device(x, y, z, k):
        return (2 * (x % 4) + z % 2, 4 * (y % 4) + 2 * (z // 2) + k)

    def along_x(step, flip=0):
        return device(x + step, y, 2 * zh + (1 - zl if flip else zl), k)

    def along_y(step):
        return device(x, y + step, z, k)

    def xs(step):
        return (x + step) % 4

    def ys(step):
        return (y + step) % 4

    zl_mate = device(x, y, 2 * zh + 1 - zl, k)
    zh_mate = device(x, y, 2 * (1 - zh) + zl, k)
    sibling = device(x, y, z, 1 - k)

    count = [0, 0]
    sent = []

    def put(src, target, dst=None):
        i = count[0]
        count[0] += 1
        copy = pltpu.make_async_remote_copy(
            src_ref=src, dst_ref=src if dst is None else dst, send_sem=send.at[i],
            recv_sem=recv.at[i], device_id=target, device_id_type=MESH,
        )
        copy.start()
        sent.append(copy)
        return copy

    def bring(src, dst):
        i = count[1]
        count[1] += 1
        copy = pltpu.make_async_copy(src, dst, local.at[i])
        copy.start()
        return copy

    get_acts = bring(acts, cols.at[x, zl])
    get_band = bring(out_grads, band)
    get_codes = [bring(codes.at[:, pl.ds(512 * i, 512)], inverse.at[i]) for i in range(16)]
    get_old = bring(old_factor, factor)

    barrier = pltpu.get_barrier_semaphore()
    partners = [along_x(step, flip) for flip in (0, 1) for step in range(4) if step or flip]
    partners += [along_y(step) for step in (1, 2, 3)] + [zh_mate, sibling]
    for partner in partners:
        pl.semaphore_signal(barrier, inc=1, device_id=partner, device_id_type=MESH)

    @pl.when(mixed)
    def _():
        for step in range(4):
            pl.semaphore_signal(
                barrier, inc=1, device_id=device(x + step, y, turned, k), device_id_type=MESH
            )

    pl.semaphore_wait(barrier, len(partners) + 4 * (zl + zh - 2 * zl * zh))

    s = {}

    def spread_y():
        for step in (1, 3, 2):
            s["spread", step] = put(acts.at[ys(step)], along_y(step), spread.at[y])

    def put_or_keep(src, dst, target, stay, i, j):
        go = pltpu.make_async_remote_copy(
            src_ref=src, dst_ref=dst, send_sem=send.at[i], recv_sem=recv.at[j],
            device_id=target, device_id_type=MESH,
        )

        @pl.when(stay)
        def _():
            pltpu.make_async_copy(src, dst, recv.at[j]).start()

        @pl.when(jnp.logical_not(stay))
        def _():
            go.start()

        maybe.append((go, stay))

    def arrived(at, j):
        pltpu.make_async_copy(at, at, recv.at[j]).wait()

    maybe = []
    turn_base = 100

    def turn(step):
        to = ys(-step)
        if step:
            s["spread", step].wait_recv()
            src = spread.at[to]
        else:
            src = acts.at[y]
        stay = jnp.logical_and(to == x, jnp.logical_not(mixed))
        put_or_keep(
            src, rows.at[k, x, zl, y], device(to, y, turned, k), stay,
            turn_base + step, turn_base + x,
        )

    def group(which, q, h=None):
        zl_of = 1 - zh if which else zh
        if h is None:
            return rows.at[k, :, zl_of, q]
        return rows.at[k, pl.ds(2 * h, 2), zl_of, q]

    def rows_y(which, h):
        at = group(which, y, h)
        if which:
            s["rows_z", h].wait_recv()
        else:
            for i in (2 * h, 2 * h + 1):
                arrived(rows.at[k, i, zh, y], turn_base + i)
            s["rows_z", h] = put(at, zh_mate)
        s["rows", which, 1, h] = put(at, along_y(1))
        s["rows", which, 3, h] = put(at, along_y(3))

    def rows_far(which, step):
        h = 0 if step == 1 else 1
        s["rows", which, step, h].wait_recv()
        s["far", which, step] = put(group(which, ys(-step), h), along_y(step))

    def rows_share(which, step):
        if step == 0:
            pass
        elif step == 2:
            s["far", which, 1].wait_recv()
            s["far", which, 3].wait_recv()
        else:
            s["rows", which, step, 0 if step == 3 else 1].wait_recv()
        at = group(which, ys(-step))
        s["share", which, step] = put(at, sibling)

    def dot(own, which, step):
        kk = k if own else 1 - k
        zl_of = 1 - zh if which else zh
        if not own:
            s["share", which, step].wait_recv()
        q = ys(-step)
        stats[kk] += tdot(
            rows[kk, :, zl_of, q].reshape(512, 512), cols[:, zl_of, q].reshape(512, 512)
        )

    def cols_half(which, step, h):
        return cols.at[xs(step), 1 - zl if which else zl, pl.ds(2 * h, 2)]

    def cols_z():
        s["cols_z"] = put(cols.at[x, zl], zl_mate)

    def cols_x(which, h):
        if which and h == 0:
            s["cols_z"].wait_recv()
        at = cols_half(which, 0, h)
        s["cols", which, 1, h] = put(at, along_x(1))
        s["cols", which, 3, h] = put(at, along_x(3))

    def cols_far(step, which=0):
        h = 0 if step == 1 else 1
        s["cols", which, step, h].wait_recv()
        s["cols_far", which, step] = put(cols_half(which, -step, h), along_x(step))

    def cols_all():
        for which in (0, 1):
            s["cols", which, 1, 1].wait_recv()
            s["cols", which, 3, 0].wait_recv()
            s["cols_far", which, 1].wait_recv()
            s["cols_far", which, 3].wait_recv()

    def part_sum():
        get_acts.wait()
        get_band.wait()
        mine = cols[x, zl].reshape(512, 512)
        for i in range(4):
            part = tdot(mine, band[:, 256 * i : 256 * i + 256]).astype(BF16)
            partial[2 * i] = part[:, :128]
            partial[2 * i + 1] = part[:, 128:]

    def rep_of(step, flip):
        return 2 * xs(step) + (1 - zl if flip else zl)

    def part(step, flip):
        s["part", step, flip] = put(
            partial.at[rep_of(step, flip)], along_x(step, flip), parts.at[r]
        )

    def grad_sum():
        total = partial[r].astype(F32)
        for step, flip in ((1, 0), (3, 0), (0, 1), (1, 1), (3, 1), (2, 0), (2, 1)):
            s["part", step, flip].wait_recv()
            total = total + parts[rep_of(-step, flip)].astype(F32)
        grad[y, zh, k] = total.astype(BF16)
        at = grad.at[y, zh, k]
        s["grad_z"] = put(at, zh_mate)
        for step in (1, 3, 2):
            s["grad", 0, step] = put(at, along_y(step))

    def grad_other():
        s["grad_z"].wait_recv()
        at = grad.at[y, 1 - zh, k]
        for step in (1, 3, 2):
            s["grad", 1, step] = put(at, along_y(step))
        at = grad.at[y, :, k]
        s["grad_share", 0] = put(at, sibling)

    def grad_share(step):
        s["grad", 0, step].wait_recv()
        s["grad", 1, step].wait_recv()
        at = grad.at[ys(-step), :, k]
        s["grad_share", step] = put(at, sibling)

    def slot(of):
        return precond.at[:, pl.ds(pl.multiple_of(128 * of, 128), 128)]

    def result():
        for i in range(4):
            s["grad_share", i].wait_recv()

        def add(i, total):
            return total + jnp.dot(
                inverse[i], grad[i // 4, (i // 2) % 2, i % 2], preferred_element_type=F32
            )

        piece[...] = lax.fori_loop(0, 16, add, jnp.zeros((512, 128), F32)).astype(BF16)
        s["keep"] = bring(piece, slot(r))
        s["out_z"] = put(piece, zl_mate, slot(r))
        for step in (1, 3, 2):
            s["out", 0, step] = put(piece, along_x(step), slot(r))

    def result_other():
        s["out_z"].wait_recv()
        at = slot(2 * x + 1 - zl)
        for step in (1, 3, 2):
            s["out", 1, step] = put(at, along_x(step))

    def result_end():
        for which in (0, 1):
            for step in (1, 3, 2):
                s["out", which, step].wait_recv()

    def dequantize(first, last):
        for i in range(first, last):
            get_codes[i].wait()

        def block(i, c):
            for u in range(4):
                for v in range(4):
                    at = (i, pl.ds(128 * u, 128), pl.ds(128 * v, 128))
                    inverse[at] = (inverse[at].astype(F32) * scales[u, 4 * i + v]).astype(BF16)
            return c

        lax.fori_loop(first, last, block, 0)

    def clear():
        stats[...] = jnp.zeros_like(stats)

    def blend(own):
        kk = k if own else 1 - k
        if own:
            get_old.wait()
        for i in range(4):
            for j in range(4):
                at = (pl.ds(512 * kk + 128 * i, 128), pl.ds(128 * j, 128))
                old = factor[at]
                new = stats[kk, pl.ds(128 * i, 128), pl.ds(128 * j, 128)]
                mixture = 0.5 * old + 0.5 * (new / 4096)
                factor[at] = jnp.where(due[j, 4 * kk + i] == 1, mixture, old)
        at = pl.ds(512 * kk, 512)
        s["leave", own] = bring(factor.at[at], new_factor.at[at])

    part_sum()
    part(1, 0)
    part(3, 0)
    part(0, 1)
    part(1, 1)
    part(3, 1)
    part(2, 0)
    part(2, 1)
    spread_y()
    cols_z()
    clear()
    dequantize(0, 8)
    turn(1)
    turn(3)
    turn(2)
    turn(0)
    dequantize(8, 16)
    grad_sum()
    cols_x(0, 0)
    cols_x(0, 1)
    rows_y(0, 0)
    rows_y(0, 1)
    rows_share(0, 0)
    grad_other()
    cols_x(1, 0)
    cols_x(1, 1)
    rows_y(1, 0)
    rows_y(1, 1)
    rows_share(1, 0)
    grad_share(1)
    grad_share(3)
    grad_share(2)
    cols_far(1)
    cols_far(3)
    rows_far(0, 1)
    rows_far(0, 3)
    result()
    rows_share(0, 1)
    rows_share(0, 3)
    cols_far(1, 1)
    cols_far(3, 1)
    rows_far(1, 1)
    rows_far(1, 3)
    result_other()
    rows_share(0, 2)
    rows_share(1, 1)
    rows_share(1, 3)
    cols_all()
    for which, step in ((0, 0), (1, 0), (0, 1), (0, 3), (0, 2), (1, 1), (1, 3)):
        dot(1, which, step)
        dot(0, which, step)
    rows_share(1, 2)
    dot(1, 1, 2)
    blend(1)
    dot(0, 1, 2)
    blend(0)
    result_end()

    for copy in sent:
        copy.wait_send()
    for go, stay in maybe:

        @pl.when(jnp.logical_not(stay))
        def _():
            go.wait_send()

    s["keep"].wait()
    s["leave", 1].wait()
    s["leave", 0].wait()


def local(acts, out_grads, codes, scales, old_factor, due):
    anywhere = pl.BlockSpec(memory_space=pl.ANY)
    scalar = pl.BlockSpec(memory_space=pltpu.SMEM)
    return pl.pallas_call(
        kernel,
        out_shape=(
            jax.ShapeDtypeStruct((512, 1024), BF16),
            jax.ShapeDtypeStruct((1024, 512), F32),
        ),
        in_specs=[anywhere, anywhere, anywhere, scalar, anywhere, scalar],
        out_specs=(anywhere, anywhere),
        scratch_shapes=[
            pltpu.VMEM((4, 2, 4, 128, 512), BF16),
            pltpu.VMEM((2, 4, 2, 4, 128, 512), BF16),
            pltpu.VMEM((4, 128, 512), BF16),
            pltpu.VMEM((512, 1024), BF16),
            pltpu.VMEM((8, 512, 128), BF16),
            pltpu.VMEM((8, 512, 128), BF16),
            pltpu.VMEM((4, 2, 2, 512, 128), BF16),
            pltpu.VMEM((16, 512, 512), BF16),
            pltpu.VMEM((1024, 512), F32),
            pltpu.VMEM((2, 512, 512), F32),
            pltpu.VMEM((512, 128), BF16),
            pltpu.SemaphoreType.DMA((104,)),
            pltpu.SemaphoreType.DMA((104,)),
            pltpu.SemaphoreType.DMA((24,)),
        ],
        compiler_params=pltpu.CompilerParams(
            collective_id=0, has_side_effects=True, vmem_limit_bytes=56 * 2**20
        ),
    )(acts.reshape(4, 128, 512), out_grads, codes, scales, old_factor, due.T)


def solution(mesh):
    return jax.shard_map(
        local,
        mesh=mesh,
        in_specs=(
            P("rep", "blk"),
            P("rep", None),
            P("blk", None),
            P("blk", None),
            P("rep", "blk"),
            P("rep", "blk"),
        ),
        out_specs=(P("blk", None), P("rep", "blk")),
        check_vma=False,
    )
```

```python
import jax
import jax.numpy as jnp
from jax import lax
from jax.experimental import pallas as pl
from jax.experimental.pallas import tpu as pltpu
from jax.sharding import PartitionSpec as P

MESH = pl.DeviceIdType.MESH
F32, BF16 = jnp.float32, jnp.bfloat16


def tdot(left, right):
    return lax.dot_general(
        left, right, (((0,), (0,)), ((), ())), preferred_element_type=F32
    )


def kernel(
    acts, out_grads, codes, scales, old_factor, due, precond, new_factor,
    cols, rows, spread, band, partial, parts, grad, inverse, factor, stats, piece,
    send, recv, local,
):
    r, b = lax.axis_index("rep"), lax.axis_index("blk")
    x, zl = r // 2, r % 2
    y, zh, k = b // 4, (b // 2) % 2, b % 2
    z = 2 * zh + zl
    turned = 2 * zl + zh
    mixed = zl != zh

    def device(x, y, z, k):
        return (2 * (x % 4) + z % 2, 4 * (y % 4) + 2 * (z // 2) + k)

    def along_x(step, flip=0):
        return device(x + step, y, 2 * zh + (1 - zl if flip else zl), k)

    def along_y(step):
        return device(x, y + step, z, k)

    def xs(step):
        return (x + step) % 4

    def ys(step):
        return (y + step) % 4

    zl_mate = device(x, y, 2 * zh + 1 - zl, k)
    zh_mate = device(x, y, 2 * (1 - zh) + zl, k)
    sibling = device(x, y, z, 1 - k)

    count = [0, 0]
    sent = []

    def put(src, target, dst=None):
        i = count[0]
        count[0] += 1
        copy = pltpu.make_async_remote_copy(
            src_ref=src, dst_ref=src if dst is None else dst, send_sem=send.at[i],
            recv_sem=recv.at[i], device_id=target, device_id_type=MESH,
        )
        copy.start()
        sent.append(copy)
        return copy

    def bring(src, dst):
        i = count[1]
        count[1] += 1
        copy = pltpu.make_async_copy(src, dst, local.at[i])
        copy.start()
        return copy

    get_acts = bring(acts, cols.at[x, zl])
    get_band = bring(out_grads, band)
    get_codes = [bring(codes.at[:, pl.ds(512 * i, 512)], inverse.at[i]) for i in range(16)]
    get_old = bring(old_factor, factor)

    barrier = pltpu.get_barrier_semaphore()
    partners = [along_x(step, flip) for flip in (0, 1) for step in range(4) if step or flip]
    partners += [along_y(step) for step in (1, 2, 3)] + [zh_mate, sibling]
    for partner in partners:
        pl.semaphore_signal(barrier, inc=1, device_id=partner, device_id_type=MESH)

    @pl.when(mixed)
    def _():
        for step in range(4):
            pl.semaphore_signal(
                barrier, inc=1, device_id=device(x + step, y, turned, k), device_id_type=MESH
            )

    pl.semaphore_wait(barrier, len(partners) + 4 * (zl + zh - 2 * zl * zh))

    s = {}

    def spread_y():
        for step in (1, 3, 2):
            s["spread", step] = put(acts.at[ys(step)], along_y(step), spread.at[y])

    def put_or_keep(src, dst, target, stay, i, j):
        go = pltpu.make_async_remote_copy(
            src_ref=src, dst_ref=dst, send_sem=send.at[i], recv_sem=recv.at[j],
            device_id=target, device_id_type=MESH,
        )

        @pl.when(stay)
        def _():
            pltpu.make_async_copy(src, dst, recv.at[j]).start()

        @pl.when(jnp.logical_not(stay))
        def _():
            go.start()

        maybe.append((go, stay))

    def arrived(at, j):
        pltpu.make_async_copy(at, at, recv.at[j]).wait()

    maybe = []
    turn_base = 100

    def turn(step):
        to = ys(-step)
        if step:
            s["spread", step].wait_recv()
            src = spread.at[to]
        else:
            src = acts.at[y]
        stay = jnp.logical_and(to == x, jnp.logical_not(mixed))
        put_or_keep(
            src, rows.at[k, x, zl, y], device(to, y, turned, k), stay,
            turn_base + step, turn_base + x,
        )

    def group(which, q, h=None):
        zl_of = 1 - zh if which else zh
        if h is None:
            return rows.at[k, :, zl_of, q]
        return rows.at[k, pl.ds(2 * h, 2), zl_of, q]

    def rows_y(which, h):
        at = group(which, y, h)
        if which:
            s["rows_z", h].wait_recv()
        else:
            for i in (2 * h, 2 * h + 1):
                arrived(rows.at[k, i, zh, y], turn_base + i)
            s["rows_z", h] = put(at, zh_mate)
        if h:
            s["rows", which, 3, 1] = put(at, along_y(3))
            s["rows", which, 1, 1] = put(at, along_y(1))
            s["rows", which, 3, 0] = put(group(which, y, 0), along_y(3))
        else:
            s["rows", which, 1, 0] = put(at, along_y(1))

    def rows_far(which, step):
        h = 0 if step == 1 else 1
        s["rows", which, step, h].wait_recv()
        s["far", which, step] = put(group(which, ys(-step), h), along_y(step))

    def rows_share(which, step):
        if step == 0:
            pass
        elif step == 2 and which:
            for way, h in ((1, 0), (3, 1)):
                s["far", which, way].wait_recv()
                at = group(which, ys(-step), h)
                s["share", which, step, h] = put(at, sibling)
            return
        elif step == 2:
            s["far", which, 1].wait_recv()
            s["far", which, 3].wait_recv()
        else:
            s["rows", which, step, 0 if step == 3 else 1].wait_recv()
        at = group(which, ys(-step))
        s["share", which, step] = put(at, sibling)

    def take(which, step):
        if which and step == 2:
            for h in (0, 1):
                s["share", which, step, h].wait_recv()
        else:
            s["share", which, step].wait_recv()

    def dot(own, zl_of, step):
        kk = k if own else 1 - k
        q = ys(-step)
        stats[kk] += tdot(
            rows[kk, :, zl_of, q].reshape(512, 512), cols[:, zl_of, q].reshape(512, 512)
        )

    def cols_half(which, step, h):
        return cols.at[xs(step), 1 - zl if which else zl, pl.ds(2 * h, 2)]

    def cols_z():
        s["cols_z"] = put(cols.at[x, zl], zl_mate)

    def cols_x(which, h):
        if which and h == 0:
            s["cols_z"].wait_recv()
        at = cols_half(which, 0, h)
        s["cols", which, 1, h] = put(at, along_x(1))
        s["cols", which, 3, h] = put(at, along_x(3))

    def cols_far(step, which=0):
        h = 0 if step == 1 else 1
        s["cols", which, step, h].wait_recv()
        s["cols_far", which, step] = put(cols_half(which, -step, h), along_x(step))

    def cols_all(which):
        s["cols", which, 1, 1].wait_recv()
        s["cols", which, 3, 0].wait_recv()
        s["cols_far", which, 1].wait_recv()
        s["cols_far", which, 3].wait_recv()

    def part_sum():
        get_acts.wait()
        get_band.wait()
        mine = cols[x, zl].reshape(512, 512)
        for i in range(4):
            part = tdot(mine, band[:, 256 * i : 256 * i + 256]).astype(BF16)
            partial[2 * i] = part[:, :128]
            partial[2 * i + 1] = part[:, 128:]

    def rep_of(step, flip):
        return 2 * xs(step) + (1 - zl if flip else zl)

    def part(step, flip):
        s["part", step, flip] = put(
            partial.at[rep_of(step, flip)], along_x(step, flip), parts.at[r]
        )

    def grad_sum():
        total = partial[r].astype(F32)
        for step, flip in ((1, 0), (3, 0), (0, 1), (1, 1), (3, 1), (2, 0), (2, 1)):
            s["part", step, flip].wait_recv()
            total = total + parts[rep_of(-step, flip)].astype(F32)
        grad[y, zh, k] = total.astype(BF16)
        at = grad.at[y, zh, k]
        s["grad_z"] = put(at, zh_mate)
        for step in (1, 3, 2):
            s["grad", 0, step] = put(at, along_y(step))

    def grad_other():
        s["grad_z"].wait_recv()
        at = grad.at[y, 1 - zh, k]
        for step in (1, 3, 2):
            s["grad", 1, step] = put(at, along_y(step))
        at = grad.at[y, :, k]
        s["grad_share", 0] = put(at, sibling)

    def grad_share(step):
        s["grad", 0, step].wait_recv()
        s["grad", 1, step].wait_recv()
        at = grad.at[ys(-step), :, k]
        s["grad_share", step] = put(at, sibling)

    def slot(of):
        return precond.at[:, pl.ds(pl.multiple_of(128 * of, 128), 128)]

    def result():
        for i in range(4):
            s["grad_share", i].wait_recv()

        def add(i, total):
            return total + jnp.dot(
                inverse[i], grad[i // 4, (i // 2) % 2, i % 2], preferred_element_type=F32
            )

        piece[...] = lax.fori_loop(0, 16, add, jnp.zeros((512, 128), F32)).astype(BF16)
        s["keep"] = bring(piece, slot(r))
        s["out_z"] = put(piece, zl_mate, slot(r))
        for step in (1, 3, 2):
            s["out", 0, step] = put(piece, along_x(step), slot(r))

    def result_other():
        s["out_z"].wait_recv()
        at = slot(2 * x + 1 - zl)
        for step in (1, 3, 2):
            s["out", 1, step] = put(at, along_x(step))

    def result_end():
        for which in (0, 1):
            for step in (1, 3, 2):
                s["out", which, step].wait_recv()

    def dequantize(first, last):
        for i in range(first, last):
            get_codes[i].wait()

        def block(i, c):
            for u in range(4):
                for v in range(4):
                    at = (i, pl.ds(128 * u, 128), pl.ds(128 * v, 128))
                    inverse[at] = (inverse[at].astype(F32) * scales[u, 4 * i + v]).astype(BF16)
            return c

        lax.fori_loop(first, last, block, 0)

    def clear():
        stats[...] = jnp.zeros_like(stats)

    def blend(own):
        kk = k if own else 1 - k
        if own:
            get_old.wait()
        for i in range(4):
            for j in range(4):
                at = (pl.ds(512 * kk + 128 * i, 128), pl.ds(128 * j, 128))
                old = factor[at]
                new = stats[kk, pl.ds(128 * i, 128), pl.ds(128 * j, 128)]
                mixture = 0.5 * old + 0.5 * (new / 4096)
                factor[at] = jnp.where(due[j, 4 * kk + i] == 1, mixture, old)
        at = pl.ds(512 * kk, 512)
        s["leave", own] = bring(factor.at[at], new_factor.at[at])

    part_sum()
    part(1, 0)
    part(3, 0)
    part(0, 1)
    part(1, 1)
    part(3, 1)
    part(2, 0)
    part(2, 1)
    spread_y()
    cols_z()
    clear()
    dequantize(0, 8)
    turn(1)
    turn(3)
    turn(2)
    turn(0)
    dequantize(8, 16)
    grad_sum()
    cols_x(0, 0)
    cols_x(0, 1)
    rows_y(0, 0)
    rows_y(0, 1)
    rows_share(0, 0)
    grad_other()
    cols_x(1, 0)
    cols_x(1, 1)
    rows_y(1, 0)
    rows_y(1, 1)
    rows_share(1, 0)
    grad_share(1)
    grad_share(3)
    grad_share(2)
    cols_far(1)
    cols_far(3)
    rows_far(0, 1)
    rows_far(0, 3)
    result()
    rows_share(0, 1)
    rows_share(0, 3)
    cols_far(1, 1)
    cols_far(3, 1)
    rows_far(1, 1)
    rows_far(1, 3)
    result_other()
    rows_share(0, 2)
    rows_share(1, 1)
    rows_share(1, 3)
    cols_all(0)
    take(0, 0)
    take(1, 0)
    dot(1, zl, 0)
    dot(0, zl, 0)
    for step in (1, 3):
        take(0, step)
        take(1, step)
        dot(1, zl, step)
        dot(0, zl, step)
    rows_share(1, 2)
    cols_all(1)
    for step in (0, 1, 3):
        dot(1, 1 - zl, step)
        dot(0, 1 - zl, step)
    take(0, 2)
    dot(1, zh, 2)
    dot(0, zh, 2)
    dot(1, 1 - zh, 2)
    blend(1)
    take(1, 2)
    dot(0, 1 - zh, 2)
    blend(0)
    result_end()

    for copy in sent:
        copy.wait_send()
    for go, stay in maybe:

        @pl.when(jnp.logical_not(stay))
        def _():
            go.wait_send()

    s["keep"].wait()
    s["leave", 1].wait()
    s["leave", 0].wait()


def local(acts, out_grads, codes, scales, old_factor, due):
    anywhere = pl.BlockSpec(memory_space=pl.ANY)
    scalar = pl.BlockSpec(memory_space=pltpu.SMEM)
    return pl.pallas_call(
        kernel,
        out_shape=(
            jax.ShapeDtypeStruct((512, 1024), BF16),
            jax.ShapeDtypeStruct((1024, 512), F32),
        ),
        in_specs=[anywhere, anywhere, anywhere, scalar, anywhere, scalar],
        out_specs=(anywhere, anywhere),
        scratch_shapes=[
            pltpu.VMEM((4, 2, 4, 128, 512), BF16),
            pltpu.VMEM((2, 4, 2, 4, 128, 512), BF16),
            pltpu.VMEM((4, 128, 512), BF16),
            pltpu.VMEM((512, 1024), BF16),
            pltpu.VMEM((8, 512, 128), BF16),
            pltpu.VMEM((8, 512, 128), BF16),
            pltpu.VMEM((4, 2, 2, 512, 128), BF16),
            pltpu.VMEM((16, 512, 512), BF16),
            pltpu.VMEM((1024, 512), F32),
            pltpu.VMEM((2, 512, 512), F32),
            pltpu.VMEM((512, 128), BF16),
            pltpu.SemaphoreType.DMA((104,)),
            pltpu.SemaphoreType.DMA((104,)),
            pltpu.SemaphoreType.DMA((24,)),
        ],
        compiler_params=pltpu.CompilerParams(
            collective_id=0, has_side_effects=True, vmem_limit_bytes=56 * 2**20
        ),
    )(acts.reshape(4, 128, 512), out_grads, codes, scales, old_factor, due.T)


def solution(mesh):
    return jax.shard_map(
        local,
        mesh=mesh,
        in_specs=(
            P("rep", "blk"),
            P("rep", None),
            P("blk", None),
            P("blk", None),
            P("rep", "blk"),
            P("rep", "blk"),
        ),
        out_specs=(P("blk", None), P("rep", "blk")),
        check_vma=False,
    )
```

```python
import jax
import jax.numpy as jnp
from jax import lax
from jax.experimental import pallas as pl
from jax.experimental.pallas import tpu as pltpu
from jax.sharding import PartitionSpec as P

MESH = pl.DeviceIdType.MESH
F32, BF16 = jnp.float32, jnp.bfloat16


def tdot(left, right):
    return lax.dot_general(
        left, right, (((0,), (0,)), ((), ())), preferred_element_type=F32
    )


def kernel(
    acts, out_grads, codes, scales, old_factor, due, precond, new_factor,
    cols, rows, spread, band, partial, parts, grad, inverse, factor, stats, piece,
    send, recv, local,
):
    r, b = lax.axis_index("rep"), lax.axis_index("blk")
    x, zl = r // 2, r % 2
    y, zh, k = b // 4, (b // 2) % 2, b % 2
    z = 2 * zh + zl
    turned = 2 * zl + zh
    mixed = zl != zh

    def device(x, y, z, k):
        return (2 * (x % 4) + z % 2, 4 * (y % 4) + 2 * (z // 2) + k)

    def along_x(step, flip=0):
        return device(x + step, y, 2 * zh + (1 - zl if flip else zl), k)

    def along_y(step):
        return device(x, y + step, z, k)

    def xs(step):
        return (x + step) % 4

    def ys(step):
        return (y + step) % 4

    zl_mate = device(x, y, 2 * zh + 1 - zl, k)
    zh_mate = device(x, y, 2 * (1 - zh) + zl, k)
    sibling = device(x, y, z, 1 - k)

    count = [0, 0]
    sent = []

    def put(src, target, dst=None):
        i = count[0]
        count[0] += 1
        copy = pltpu.make_async_remote_copy(
            src_ref=src, dst_ref=src if dst is None else dst, send_sem=send.at[i],
            recv_sem=recv.at[i], device_id=target, device_id_type=MESH,
        )
        copy.start()
        sent.append(copy)
        return copy

    def bring(src, dst):
        i = count[1]
        count[1] += 1
        copy = pltpu.make_async_copy(src, dst, local.at[i])
        copy.start()
        return copy

    get_acts = bring(acts, cols.at[x, zl])
    get_band = bring(out_grads, band)
    get_codes = [bring(codes.at[:, pl.ds(512 * i, 512)], inverse.at[i]) for i in range(16)]
    get_old = bring(old_factor, factor)

    barrier = pltpu.get_barrier_semaphore()
    partners = [along_x(step, flip) for flip in (0, 1) for step in range(4) if step or flip]
    partners += [along_y(step) for step in (1, 2, 3)] + [zh_mate, sibling]
    for partner in partners:
        pl.semaphore_signal(barrier, inc=1, device_id=partner, device_id_type=MESH)

    @pl.when(mixed)
    def _():
        for step in range(4):
            pl.semaphore_signal(
                barrier, inc=1, device_id=device(x + step, y, turned, k), device_id_type=MESH
            )

    pl.semaphore_wait(barrier, len(partners) + 4 * (zl + zh - 2 * zl * zh))

    s = {}

    def spread_y():
        for step in (1, 3, 2):
            s["spread", step] = put(acts.at[ys(step)], along_y(step), spread.at[y])

    def put_or_keep(src, dst, target, stay, i, j):
        go = pltpu.make_async_remote_copy(
            src_ref=src, dst_ref=dst, send_sem=send.at[i], recv_sem=recv.at[j],
            device_id=target, device_id_type=MESH,
        )

        @pl.when(stay)
        def _():
            pltpu.make_async_copy(src, dst, recv.at[j]).start()

        @pl.when(jnp.logical_not(stay))
        def _():
            go.start()

        maybe.append((go, stay))

    def arrived(at, j):
        pltpu.make_async_copy(at, at, recv.at[j]).wait()

    maybe = []
    turn_base = 100

    def turn(step):
        to = ys(-step)
        if step:
            s["spread", step].wait_recv()
            src = spread.at[to]
        else:
            src = acts.at[y]
        stay = jnp.logical_and(to == x, jnp.logical_not(mixed))
        put_or_keep(
            src, rows.at[k, x, zl, y], device(to, y, turned, k), stay,
            turn_base + step, turn_base + x,
        )

    def group(which, q, h=None):
        zl_of = 1 - zh if which else zh
        if h is None:
            return rows.at[k, :, zl_of, q]
        return rows.at[k, pl.ds(2 * h, 2), zl_of, q]

    def rows_y(which, h):
        at = group(which, y, h)
        if which:
            s["rows_z", h].wait_recv()
        else:
            for i in (2 * h, 2 * h + 1):
                arrived(rows.at[k, i, zh, y], turn_base + i)
            s["rows_z", h] = put(at, zh_mate)
        if h:
            s["rows", which, 3, 1] = put(at, along_y(3))
            s["rows", which, 1, 1] = put(at, along_y(1))
            s["rows", which, 3, 0] = put(group(which, y, 0), along_y(3))
        else:
            s["rows", which, 1, 0] = put(at, along_y(1))

    def rows_far(which, step):
        h = 0 if step == 1 else 1
        s["rows", which, step, h].wait_recv()
        s["far", which, step] = put(group(which, ys(-step), h), along_y(step))

    def rows_share(which, step):
        if step == 0:
            pass
        elif step == 2 and which:
            for way, h in ((1, 0), (3, 1)):
                s["far", which, way].wait_recv()
                at = group(which, ys(-step), h)
                s["share", which, step, h] = put(at, sibling)
            return
        elif step == 2:
            s["far", which, 1].wait_recv()
            s["far", which, 3].wait_recv()
        else:
            s["rows", which, step, 0 if step == 3 else 1].wait_recv()
        at = group(which, ys(-step))
        s["share", which, step] = put(at, sibling)

    def take(which, step):
        if which and step == 2:
            for h in (0, 1):
                s["share", which, step, h].wait_recv()
        else:
            s["share", which, step].wait_recv()

    def dot(own, zl_of, step):
        kk = k if own else 1 - k
        q = ys(-step)
        stats[kk] += tdot(
            rows[kk, :, zl_of, q].reshape(512, 512), cols[:, zl_of, q].reshape(512, 512)
        )

    def cols_half(which, step, h):
        return cols.at[xs(step), 1 - zl if which else zl, pl.ds(2 * h, 2)]

    def cols_z():
        s["cols_z"] = put(cols.at[x, zl], zl_mate)

    def cols_x(which, h):
        if which and h == 0:
            s["cols_z"].wait_recv()
        at = cols_half(which, 0, h)
        if h:
            s["cols", which, 3, 1] = put(at, along_x(3))
            s["cols", which, 1, 1] = put(at, along_x(1))
            s["cols", which, 3, 0] = put(cols_half(which, 0, 0), along_x(3))
        else:
            s["cols", which, 1, 0] = put(at, along_x(1))

    def cols_far(step, which=0):
        h = 0 if step == 1 else 1
        s["cols", which, step, h].wait_recv()
        s["cols_far", which, step] = put(cols_half(which, -step, h), along_x(step))

    def cols_all(which):
        s["cols", which, 1, 1].wait_recv()
        s["cols", which, 3, 0].wait_recv()
        s["cols_far", which, 1].wait_recv()
        s["cols_far", which, 3].wait_recv()

    def part_sum():
        get_acts.wait()
        get_band.wait()
        mine = cols[x, zl].reshape(512, 512)
        for i in range(4):
            part = tdot(mine, band[:, 256 * i : 256 * i + 256]).astype(BF16)
            partial[2 * i] = part[:, :128]
            partial[2 * i + 1] = part[:, 128:]

    def rep_of(step, flip):
        return 2 * xs(step) + (1 - zl if flip else zl)

    def part(step, flip):
        s["part", step, flip] = put(
            partial.at[rep_of(step, flip)], along_x(step, flip), parts.at[r]
        )

    def grad_sum():
        total = partial[r].astype(F32)
        for step, flip in ((1, 0), (3, 0), (0, 1), (1, 1), (3, 1), (2, 0), (2, 1)):
            s["part", step, flip].wait_recv()
            total = total + parts[rep_of(-step, flip)].astype(F32)
        grad[y, zh, k] = total.astype(BF16)
        at = grad.at[y, zh, k]
        s["grad_z"] = put(at, zh_mate)
        for step in (1, 3, 2):
            s["grad", 0, step] = put(at, along_y(step))

    def grad_other():
        s["grad_z"].wait_recv()
        at = grad.at[y, 1 - zh, k]
        for step in (1, 3, 2):
            s["grad", 1, step] = put(at, along_y(step))
        at = grad.at[y, :, k]
        s["grad_share", 0] = put(at, sibling)

    def grad_share(step):
        s["grad", 0, step].wait_recv()
        s["grad", 1, step].wait_recv()
        at = grad.at[ys(-step), :, k]
        s["grad_share", step] = put(at, sibling)

    def slot(of):
        return precond.at[:, pl.ds(pl.multiple_of(128 * of, 128), 128)]

    def result():
        for i in range(4):
            s["grad_share", i].wait_recv()

        def add(i, total):
            return total + jnp.dot(
                inverse[i], grad[i // 4, (i // 2) % 2, i % 2], preferred_element_type=F32
            )

        piece[...] = lax.fori_loop(0, 16, add, jnp.zeros((512, 128), F32)).astype(BF16)
        s["keep"] = bring(piece, slot(r))
        s["out_z"] = put(piece, zl_mate, slot(r))
        for step in (1, 3, 2):
            s["out", 0, step] = put(piece, along_x(step), slot(r))

    def result_other():
        s["out_z"].wait_recv()
        at = slot(2 * x + 1 - zl)
        for step in (1, 3, 2):
            s["out", 1, step] = put(at, along_x(step))

    def result_end():
        for which in (0, 1):
            for step in (1, 3, 2):
                s["out", which, step].wait_recv()

    def dequantize(first, last):
        for i in range(first, last):
            get_codes[i].wait()

        def block(i, c):
            for u in range(4):
                for v in range(4):
                    at = (i, pl.ds(128 * u, 128), pl.ds(128 * v, 128))
                    inverse[at] = (inverse[at].astype(F32) * scales[u, 4 * i + v]).astype(BF16)
            return c

        lax.fori_loop(first, last, block, 0)

    def clear():
        stats[...] = jnp.zeros_like(stats)

    def blend(own):
        kk = k if own else 1 - k
        if own:
            get_old.wait()
        for i in range(4):
            for j in range(4):
                at = (pl.ds(512 * kk + 128 * i, 128), pl.ds(128 * j, 128))
                old = factor[at]
                new = stats[kk, pl.ds(128 * i, 128), pl.ds(128 * j, 128)]
                mixture = 0.5 * old + 0.5 * (new / 4096)
                factor[at] = jnp.where(due[j, 4 * kk + i] == 1, mixture, old)
        at = pl.ds(512 * kk, 512)
        s["leave", own] = bring(factor.at[at], new_factor.at[at])

    part_sum()
    part(1, 0)
    part(3, 0)
    part(0, 1)
    part(1, 1)
    part(3, 1)
    part(2, 0)
    part(2, 1)
    spread_y()
    cols_z()
    clear()
    dequantize(0, 8)
    turn(1)
    turn(3)
    turn(2)
    turn(0)
    dequantize(8, 16)
    grad_sum()
    cols_x(0, 0)
    cols_x(0, 1)
    rows_y(0, 0)
    rows_y(0, 1)
    rows_share(0, 0)
    grad_other()
    cols_x(1, 0)
    cols_x(1, 1)
    rows_y(1, 0)
    rows_y(1, 1)
    rows_share(1, 0)
    grad_share(1)
    grad_share(3)
    grad_share(2)
    cols_far(1)
    cols_far(3)
    rows_far(0, 1)
    rows_far(0, 3)
    result()
    rows_share(0, 1)
    rows_share(0, 3)
    cols_far(1, 1)
    cols_far(3, 1)
    rows_far(1, 1)
    rows_far(1, 3)
    result_other()
    rows_share(0, 2)
    rows_share(1, 1)
    rows_share(1, 3)
    cols_all(0)
    take(0, 0)
    take(1, 0)
    dot(1, zl, 0)
    dot(0, zl, 0)
    for step in (1, 3):
        take(0, step)
        take(1, step)
        dot(1, zl, step)
        dot(0, zl, step)
    rows_share(1, 2)
    cols_all(1)
    for step in (0, 1, 3):
        dot(1, 1 - zl, step)
        dot(0, 1 - zl, step)
    take(0, 2)
    dot(1, zh, 2)
    dot(0, zh, 2)
    dot(1, 1 - zh, 2)
    blend(1)
    take(1, 2)
    dot(0, 1 - zh, 2)
    blend(0)
    result_end()

    for copy in sent:
        copy.wait_send()
    for go, stay in maybe:

        @pl.when(jnp.logical_not(stay))
        def _():
            go.wait_send()

    s["keep"].wait()
    s["leave", 1].wait()
    s["leave", 0].wait()


def local(acts, out_grads, codes, scales, old_factor, due):
    anywhere = pl.BlockSpec(memory_space=pl.ANY)
    scalar = pl.BlockSpec(memory_space=pltpu.SMEM)
    return pl.pallas_call(
        kernel,
        out_shape=(
            jax.ShapeDtypeStruct((512, 1024), BF16),
            jax.ShapeDtypeStruct((1024, 512), F32),
        ),
        in_specs=[anywhere, anywhere, anywhere, scalar, anywhere, scalar],
        out_specs=(anywhere, anywhere),
        scratch_shapes=[
            pltpu.VMEM((4, 2, 4, 128, 512), BF16),
            pltpu.VMEM((2, 4, 2, 4, 128, 512), BF16),
            pltpu.VMEM((4, 128, 512), BF16),
            pltpu.VMEM((512, 1024), BF16),
            pltpu.VMEM((8, 512, 128), BF16),
            pltpu.VMEM((8, 512, 128), BF16),
            pltpu.VMEM((4, 2, 2, 512, 128), BF16),
            pltpu.VMEM((16, 512, 512), BF16),
            pltpu.VMEM((1024, 512), F32),
            pltpu.VMEM((2, 512, 512), F32),
            pltpu.VMEM((512, 128), BF16),
            pltpu.SemaphoreType.DMA((104,)),
            pltpu.SemaphoreType.DMA((104,)),
            pltpu.SemaphoreType.DMA((24,)),
        ],
        compiler_params=pltpu.CompilerParams(
            collective_id=0, has_side_effects=True, vmem_limit_bytes=56 * 2**20
        ),
    )(acts.reshape(4, 128, 512), out_grads, codes, scales, old_factor, due.T)


def solution(mesh):
    return jax.shard_map(
        local,
        mesh=mesh,
        in_specs=(
            P("rep", "blk"),
            P("rep", None),
            P("blk", None),
            P("blk", None),
            P("rep", "blk"),
            P("rep", "blk"),
        ),
        out_specs=(P("blk", None), P("rep", "blk")),
        check_vma=False,
    )
```
